512 devices in a mesh: grp: 16 (over y, x_hi), blk: 32 (over x_lo, z, core).
Axes of the slice: x: 4 (x_hi: 2, x_lo: 2; x = x_hi * 2 + x_lo), y: 8, z: 8, core: 2. Of those that a mesh axis runs over, the one named last changes fastest.
Arguments:
- images: bfloat16 [65536, 1152], P(('grp', 'blk')), may hold values from -6 to 6
- texts: bfloat16 [65536, 1152], P(('grp', 'blk')), may hold values from -6 to 6
- log_temp: float32 [1], replicated, may hold values from 2 to 2.7
- bias: float32 [1], replicated, may hold values from -3 to -1
Outputs:
- image_grad: float32 [65536, 1152], P(('grp', 'blk'))
- text_grad: float32 [65536, 1152], P(('grp', 'blk'))
The draws below stay inside these ranges and needn't reach their ends.
All inputs are finite; a program needn't handle non-finite values.
Results may differ from the reference program's by a relative error of at most 0.0055.
Values may be sent and summed in bfloat16 or wider, within the bound.
A program may use at most 64 MiB of HBM per device.

```python
import jax
import jax.numpy as jnp
from jax import lax

D = 1152
ROWS = 128
HOPS = 2
BATCH = 65536
N_GRP = 16
N_BLK = 32


def steps_of(rng, dims, cuts, least, largest):
    def one(axis_at, parts):
        draws = jax.random.uniform(jax.random.fold_in(jax.random.fold_in(rng, 6), axis_at), (parts,), jnp.float32, least / len(cuts), largest / len(cuts))
        return jnp.repeat(jnp.exp(draws), dims[axis_at] // parts).reshape((-1,) + (1,) * (len(dims) - axis_at - 1))

    loudness = one(*cuts[0])
    for cut in cuts[1:]:
        loudness = loudness * one(*cut)
    return loudness


def bell_draw(own_key, extent, scale, limit, cuts=(), kind=jnp.bfloat16):
    values = jax.random.normal(own_key, extent, jnp.float32) * scale
    if len(cuts) > 0:
        values = steps_of(own_key, extent, cuts, -0.22, 0.18) * values
    return jnp.clip(values, min=-limit, max=limit).astype(kind)


def setup_inputs(seed: int = 0) -> dict:
    key_list = jax.random.split(jax.random.key(seed), 5)
    return {
        "images": bell_draw(key_list[0], (BATCH, D), 1.0, 6.0, ((0, 512),)),
        "texts": bell_draw(key_list[1], (BATCH, D), 1.0, 6.0, ((0, 512),)),
        "log_temp": jnp.clip(jax.random.uniform(key_list[2], (1,), jnp.float32, 2.0, 2.7), 2.0, 2.7),
        "bias": jnp.clip(jax.random.uniform(key_list[3], (1,), jnp.float32, -3.0, -1.0), -3.0, -1.0),
    }


def unit_rows(values):
    wide = values.astype(jnp.float32)
    norms = jnp.sqrt(lax.optimization_barrier(jnp.sum(wide * wide, axis=1, keepdims=True)) + 1e-06)
    return (wide / norms, norms)

def back_rows(unit, norms, upstream):
    inner = lax.optimization_barrier(jnp.sum(unit * upstream, axis=1, keepdims=True))
    return (upstream - unit * inner) / norms

def reference(images, texts, log_temp, bias):
    img_unit, img_norm = unit_rows(images)
    txt_unit, txt_norm = unit_rows(texts)
    img_half = img_unit.astype(jnp.bfloat16)
    txt_half = txt_unit.astype(jnp.bfloat16)
    scale = jnp.exp(log_temp[0])
    offset = bias[0]
    width = images.shape[1]
    img_four = img_half.astype(jnp.float32).reshape(N_GRP, N_BLK, ROWS, width)
    txt_four = txt_half.astype(jnp.float32).reshape(N_GRP, N_BLK, ROWS, width)
    span = N_GRP * ROWS
    img_cols = jnp.transpose(img_four, (1, 0, 2, 3)).reshape(N_BLK, span, width)
    txt_cols = jnp.transpose(txt_four, (1, 0, 2, 3)).reshape(N_BLK, span, width)
    row_ids = lax.broadcasted_iota(jnp.int32, (span, span), 0)
    col_ids = lax.broadcasted_iota(jnp.int32, (span, span), 1)
    sign = jnp.where(row_ids == col_ids, jnp.float32(1.0), jnp.float32(-1.0))

    def block_part(pair):
        img_rows, txt_rows = pair
        logits = scale * jnp.dot(img_rows, txt_rows.T) + offset
        coef = (-sign * jax.nn.sigmoid(-sign * logits) * scale).astype(jnp.bfloat16).astype(jnp.float32)
        return (jnp.dot(coef, txt_rows), jnp.dot(coef.T, img_rows))
    img_part, txt_part = lax.map(block_part, (img_cols, txt_cols))
    img_grad = jnp.transpose(img_part.reshape(N_BLK, N_GRP, ROWS, width), (1, 0, 2, 3))
    txt_grad = jnp.transpose(txt_part.reshape(N_BLK, N_GRP, ROWS, width), (1, 0, 2, 3))
    for hop in range(1, HOPS + 1):
        for direction in (1, -1):
            moved = jnp.roll(txt_four, direction * hop, axis=1)
            logits = scale * jnp.einsum('gbid,gbjd->gbij', img_four, moved) + offset
            coef = (jax.nn.sigmoid(logits) * scale).astype(jnp.bfloat16).astype(jnp.float32)
            img_grad = img_grad + jnp.einsum('gbij,gbjd->gbid', coef, moved)
            back = jnp.einsum('gbij,gbid->gbjd', coef, img_four)
            txt_grad = txt_grad + jnp.roll(back, -direction * hop, axis=1)
    img_grad = img_grad.reshape(-1, width)
    txt_grad = txt_grad.reshape(-1, width)
    return (back_rows(img_unit, img_norm, img_grad), back_rows(txt_unit, txt_norm, txt_grad))
```

```python
import jax
import jax.numpy as jnp
from jax import lax
from jax.experimental import pallas as pl
from jax.experimental.pallas import tpu as pltpu
from jax.sharding import PartitionSpec as P

MESH = pl.DeviceIdType.MESH
ROWS = 128
D = 1152
HALF = 64
RING = 8
OFFSETS = (1, -1, 2, -2)

F32 = jnp.float32
BF16 = jnp.bfloat16


def dot_nt(a, b):
    return lax.dot_general(a, b, (((1,), (1,)), ((), ())), preferred_element_type=F32)


def dot_nn(a, b):
    return jnp.dot(a, b, preferred_element_type=F32)


def rows_norm(values):
    wide = values.astype(F32)
    return jnp.sqrt(jnp.sum(wide * wide, axis=1, keepdims=True) + 1e-06)


def back_rows(values, norms, upstream):
    rcp = 1.0 / norms
    unit = values.astype(F32) * rcp
    inner = jnp.sum(unit * upstream, axis=1, keepdims=True)
    return (upstream - unit * inner) * rcp


def kernel(
    temp_ref,
    bias_ref,
    img_ref,
    txt_ref,
    gi_ref,
    gt_ref,
    own_txt,
    imgs,
    ring,
    far,
    near_img,
    near_txt,
    img_acc,
    txt_acc,
    part,
    part_far,
    out_l,
    out_r,
    in_l,
    in_r,
    img_out,
    img_in,
    norms,
    sems,
):
    g = lax.axis_index("grp")
    b = lax.axis_index("blk")
    n_grp = lax.axis_size("grp")
    n_blk = lax.axis_size("blk")
    fore = ((g + 2) % n_grp, b)
    back = ((g + n_grp - 2) % n_grp, b)
    mate = (g + 1 - 2 * (g % 2), b)
    near = [(g, (b + n_blk + o) % n_blk) for o in OFFSETS]

    barrier = pltpu.get_barrier_semaphore()
    for dev in [fore, back, mate] + near:
        pl.semaphore_signal(barrier, inc=1, device_id=dev, device_id_type=MESH)

    scale = jnp.exp(jnp.full((1, 1), temp_ref[0], F32))
    offset = bias_ref[0]

    pending = []
    count = [0]

    def send(src, dst, dev):
        i = count[0]
        count[0] += 1
        copy = pltpu.make_async_remote_copy(
            src_ref=src,
            dst_ref=dst,
            send_sem=sems.at[0, i],
            recv_sem=sems.at[1, i],
            device_id=dev,
            device_id_type=MESH,
        )
        copy.start()
        pending.append(copy)
        return copy

    def half(h):
        return pl.ds(h * HALF, HALF)

    tn = rows_norm(txt_ref[...])
    norms[1] = tn
    own_txt[...] = (txt_ref[...].astype(F32) * (1.0 / tn)).astype(BF16)
    pl.semaphore_wait(barrier, 7)

    gather_f = {}
    gather_b = {}
    for h in range(2):
        gather_f[1, h] = send(own_txt.at[half(h)], ring.at[0, half(h)], fore)
        gather_b[1, h] = send(own_txt.at[half(h)], ring.at[0, pl.ds(ROWS + h * HALF, HALF)], back)

    im = rows_norm(img_ref[...])
    norms[0] = im
    imgs[0:ROWS] = (img_ref[...].astype(F32) * (1.0 / im)).astype(BF16)
    mate_copy = send(imgs.at[pl.ds(0, ROWS)], imgs.at[pl.ds(ROWS, ROWS)], mate)

    def forward(k):
        for h in range(2):
            f = (k + 1, h)
            gather_f[k, h].wait_recv()
            if k < 3:
                gather_f[f] = send(ring.at[k - 1, half(h)], ring.at[k, half(h)], fore)
            elif h == 0:
                gather_f[f] = send(ring.at[k - 1, half(0)], far.at[half(0)], fore)
            gather_b[k, h].wait_recv()
            up = pl.ds(ROWS + h * HALF, HALF)
            if k < 3:
                gather_b[f] = send(ring.at[k - 1, up], ring.at[k, up], back)
            elif h == 1:
                gather_b[f] = send(ring.at[k - 1, up], far.at[half(1)], back)

    def negative(logits):
        return (jax.nn.sigmoid(logits) * scale).astype(BF16)

    def score(a, c):
        return scale * dot_nt(a, c) + offset

    def ring_step(k):
        texts = ring[k - 1]
        pair = imgs[...]
        coef = negative(score(pair, texts))
        img_acc[...] += dot_nn(coef, texts)
        part[k - 1] = dot_nn(coef.T, pair)

    forward(1)
    forward(2)
    mate_copy.wait_recv()

    near_copies = []
    for i, dev in enumerate(near):
        near_copies.append(send(imgs.at[pl.ds(0, ROWS)], near_img.at[pl.ds(i * ROWS, ROWS)], dev))
        near_copies.append(send(own_txt, near_txt.at[pl.ds(i * ROWS, ROWS)], dev))

    texts = own_txt[...]
    pair = imgs[...]
    logits = score(pair, texts)
    same = lax.broadcasted_iota(jnp.int32, logits.shape, 0) == lax.broadcasted_iota(
        jnp.int32, logits.shape, 1
    )
    sign = jnp.where(same, jnp.float32(1.0), jnp.float32(-1.0))
    coef = (-sign * jax.nn.sigmoid(-sign * logits) * scale).astype(BF16)
    img_acc[...] = dot_nn(coef, texts)
    txt_acc[...] = dot_nn(coef.T, pair)
    ring_step(1)
    ring_step(2)

    forward(3)
    ring_step(3)

    sums_l = {}
    sums_r = {}

    def give_l(k, h, value):
        out_l[k - 1, half(h)] = value.astype(BF16)
        sums_l[k - 1, h] = send(out_l.at[k - 1, half(h)], in_l.at[k - 1, half(h)], back)

    def give_r(k, h, value):
        out_r[k - 1, half(h)] = value.astype(BF16)
        sums_r[k - 1, h] = send(out_r.at[k - 1, half(h)], in_r.at[k - 1, half(h)], fore)

    def mine_l(k, h):
        return part[k - 1, half(h)]

    def mine_r(k, h):
        return part[k - 1, pl.ds(ROWS + h * HALF, HALF)]

    give_l(3, 1, mine_l(3, 1))
    give_r(3, 0, mine_r(3, 0))

    gather_f[4, 0].wait_recv()
    gather_b[4, 1].wait_recv()
    texts = far[...]
    pair = imgs[...]
    coef = negative(score(pair, texts))
    part_far[...] = dot_nn(coef.T, pair)
    give_l(4, 0, part_far[half(0)])
    give_r(4, 1, part_far[half(1)])
    img_acc[...] += dot_nn(coef, texts)
    img_out[...] = img_acc[ROWS : 2 * ROWS].astype(BF16)
    img_back = send(img_out, img_in, mate)

    def relay(k, h):
        sums_l[k, h].wait_recv()
        give_l(k, h, mine_l(k, h) + in_l[k, half(h)].astype(F32))
        q = 1 - h
        sums_r[k, q].wait_recv()
        give_r(k, q, mine_r(k, q) + in_r[k, half(q)].astype(F32))

    relay(2, 1)
    relay(3, 0)
    relay(1, 1)
    relay(2, 0)

    for copy in near_copies:
        copy.wait_recv()
    texts = near_txt[...]
    coef = negative(score(imgs[0:ROWS], texts))
    img_acc[0:ROWS] += dot_nn(coef, texts)
    relay(1, 0)

    others = near_img[...]
    coef = negative(score(own_txt[...], others))
    txt_acc[...] += dot_nn(coef, others)

    img_back.wait_recv()
    gi_ref[...] = back_rows(
        img_ref[...], norms[0], img_acc[0:ROWS] + img_in[...].astype(F32)
    )

    sums_l[0, 1].wait_recv()
    sums_r[0, 0].wait_recv()
    sums_l[0, 0].wait_recv()
    sums_r[0, 1].wait_recv()
    gt_ref[...] = back_rows(
        txt_ref[...],
        norms[1],
        txt_acc[...] + in_l[0].astype(F32) + in_r[0].astype(F32),
    )
    for copy in pending:
        copy.wait_send()


def per_device(images, texts, log_temp, bias):
    vmem = pl.BlockSpec(memory_space=pltpu.VMEM)
    smem = pl.BlockSpec(memory_space=pltpu.SMEM)
    out = jax.ShapeDtypeStruct((ROWS, D), F32)
    return pl.pallas_call(
        kernel,
        out_shape=(out, out),
        in_specs=[smem, smem, vmem, vmem],
        out_specs=(vmem, vmem),
        scratch_shapes=[
            pltpu.VMEM((ROWS, D), BF16),
            pltpu.VMEM((2 * ROWS, D), BF16),
            pltpu.VMEM((3, 2 * ROWS, D), BF16),
            pltpu.VMEM((ROWS, D), BF16),
            pltpu.VMEM((4 * ROWS, D), BF16),
            pltpu.VMEM((4 * ROWS, D), BF16),
            pltpu.VMEM((2 * ROWS, D), F32),
            pltpu.VMEM((ROWS, D), F32),
            pltpu.VMEM((3, 2 * ROWS, D), F32),
            pltpu.VMEM((ROWS, D), F32),
            pltpu.VMEM((4, ROWS, D), BF16),
            pltpu.VMEM((4, ROWS, D), BF16),
            pltpu.VMEM((4, ROWS, D), BF16),
            pltpu.VMEM((4, ROWS, D), BF16),
            pltpu.VMEM((ROWS, D), BF16),
            pltpu.VMEM((ROWS, D), BF16),
            pltpu.VMEM((2, ROWS, 1), F32),
            pltpu.SemaphoreType.DMA((2, 40)),
        ],
        compiler_params=pltpu.CompilerParams(
            collective_id=0, has_side_effects=True, vmem_limit_bytes=40 * 1024 * 1024
        ),
        cost_estimate=pl.CostEstimate(
            flops=2_600_000_000, bytes_accessed=2_000_000, transcendentals=500_000
        ),
    )(log_temp, bias, images, texts)


def solution(mesh):
    return jax.shard_map(
        per_device,
        mesh=mesh,
        in_specs=(P(("grp", "blk"), None), P(("grp", "blk"), None), P(), P()),
        out_specs=(P(("grp", "blk"), None), P(("grp", "blk"), None)),
        check_vma=False,
    )
```

```python
import jax
import jax.numpy as jnp
from jax import lax
from jax.experimental import pallas as pl
from jax.experimental.pallas import tpu as pltpu
from jax.sharding import PartitionSpec as P

MESH = pl.DeviceIdType.MESH
ROWS = 128
D = 1152
C = 4
H = C // 2
R = ROWS // C
OFFSETS = (1, -1, 2, -2)

F32 = jnp.float32
BF16 = jnp.bfloat16


def dot_nt(a, b):
    return lax.dot_general(a, b, (((1,), (1,)), ((), ())), preferred_element_type=F32)


def dot_nn(a, b):
    return jnp.dot(a, b, preferred_element_type=F32)


def rows_norm(values):
    wide = values.astype(F32)
    return jnp.sqrt(jnp.sum(wide * wide, axis=1, keepdims=True) + 1e-06)


def unit_half(values):
    return (values.astype(F32) * (1.0 / rows_norm(values))).astype(BF16)


def back_rows(values, norms, upstream):
    rcp = 1.0 / norms
    unit = values.astype(F32) * rcp
    inner = jnp.sum(unit * upstream, axis=1, keepdims=True)
    return (upstream - unit * inner) * rcp


def rank(b):
    return jnp.where((b // 2) % 8 == 0, 0, 1000) + (b % 2) * 100 + b


def chunk(c):
    return pl.ds(c * R, R)


def kernel(
    temp_ref,
    bias_ref,
    img_ref,
    txt_ref,
    gi_ref,
    gt_ref,
    img_v,
    txt_v,
    own_txt,
    mate_raw,
    imgs,
    ring,
    ring_half,
    far,
    near_img,
    near_txt,
    img_acc,
    txt_acc,
    part,
    part_far,
    out_l,
    out_r,
    in_l,
    in_r,
    img_out,
    img_in,
    norms,
    local_sems,
    sems,
    ready,
):
    g = lax.axis_index("grp")
    b = lax.axis_index("blk")
    n_grp = lax.axis_size("grp")
    n_blk = lax.axis_size("blk")
    fore = ((g + 2) % n_grp, b)
    back = ((g + n_grp - 2) % n_grp, b)
    mate = (g + 1 - 2 * (g % 2), b)
    near_blk = [(b + n_blk + o) % n_blk for o in OFFSETS]
    near = [(g, n) for n in near_blk]
    earlier = [rank(n) < rank(b) for n in near_blk]

    loads = []
    for i, (src, dst) in enumerate(((txt_ref, txt_v), (img_ref, img_v))):
        load = pltpu.make_async_copy(src, dst, local_sems.at[i])
        load.start()
        loads.append(load)

    barrier = pltpu.get_barrier_semaphore()
    for dev in (fore, back, mate):
        pl.semaphore_signal(barrier, inc=1, device_id=dev, device_id_type=MESH)
    greeted = 3
    for dev, known in zip(near, earlier):

        @pl.when(jnp.logical_not(known))
        def _():
            pl.semaphore_signal(barrier, inc=1, device_id=dev, device_id_type=MESH)

        greeted = greeted + known.astype(jnp.int32)
    pl.semaphore_wait(barrier, greeted)

    pending = []
    count = [0]

    def prepare(src, dst, dev):
        i = count[0]
        count[0] += 1
        copy = pltpu.make_async_remote_copy(
            src_ref=src,
            dst_ref=dst,
            send_sem=sems.at[0, i],
            recv_sem=sems.at[1, i],
            device_id=dev,
            device_id_type=MESH,
        )
        pending.append(copy)
        return copy

    def send(src, dst, dev):
        copy = prepare(src, dst, dev)
        copy.start()
        return copy

    def upper(c):
        return pl.ds(ROWS + c * R, R)

    gather_f = {}
    gather_b = {}
    for c in range(C):
        d = C - 1 - c
        gather_f[1, c] = send(txt_ref.at[chunk(c)], ring.at[0, chunk(c)], fore)
        gather_b[1, d] = send(txt_ref.at[chunk(d)], ring.at[0, upper(d)], back)
    mate_copy = send(img_ref, mate_raw, mate)
    for dev, known in zip(near, earlier):

        @pl.when(known)
        def _():
            pl.semaphore_signal(ready, inc=1, device_id=dev, device_id_type=MESH)

    for load in loads:
        load.wait()
    norms[1] = rows_norm(txt_v[...])
    own_txt[...] = (txt_v[...].astype(F32) * (1.0 / norms[1])).astype(BF16)
    norms[0] = rows_norm(img_v[...])
    imgs[0:ROWS] = (img_v[...].astype(F32) * (1.0 / norms[0])).astype(BF16)
    scale = jnp.exp(temp_ref[...])
    offset = bias_ref[...]

    near_copies = []
    for i, dev in enumerate(near):
        rows = pl.ds(i * ROWS, ROWS)
        near_copies.append(prepare(imgs.at[pl.ds(0, ROWS)], near_img.at[rows], dev))
        near_copies.append(prepare(own_txt, near_txt.at[rows], dev))

    def send_near(which):
        for i in range(len(OFFSETS)):

            @pl.when(which[i])
            def _():
                near_copies[2 * i].start()
                near_copies[2 * i + 1].start()

    def forward(k, c):
        d = C - 1 - c
        gather_f[k, c].wait_recv()
        if k < 3:
            gather_f[k + 1, c] = send(ring.at[k - 1, chunk(c)], ring.at[k, chunk(c)], fore)
        elif c < H:
            gather_f[4, c] = send(ring.at[k - 1, chunk(c)], far.at[chunk(c)], fore)
        gather_b[k, d].wait_recv()
        if k < 3:
            gather_b[k + 1, d] = send(ring.at[k - 1, upper(d)], ring.at[k, upper(d)], back)
        elif d >= H:
            gather_b[4, d] = send(ring.at[k - 1, upper(d)], far.at[chunk(d)], back)

    def negative(logits):
        return (jax.nn.sigmoid(logits) * scale).astype(BF16)

    def score(a, c):
        return scale * dot_nt(a, c) + offset

    def ring_step(k):
        ring_half[...] = unit_half(ring[k - 1])
        texts = ring_half[...]
        pair = imgs[...]
        coef = negative(score(pair, texts))
        part[k - 1] = dot_nn(coef.T, pair)
        img_acc[...] += dot_nn(coef, texts)

    def own_step():
        texts = own_txt[...]
        pair = imgs[...]
        logits = score(pair, texts)
        same = lax.broadcasted_iota(jnp.int32, logits.shape, 0) == lax.broadcasted_iota(
            jnp.int32, logits.shape, 1
        )
        sign = jnp.where(same, jnp.float32(1.0), jnp.float32(-1.0))
        coef = (-sign * jax.nn.sigmoid(-sign * logits) * scale).astype(BF16)
        img_acc[...] = dot_nn(coef, texts)
        txt_acc[...] = dot_nn(coef.T, pair)

    for c in range(C):
        forward(1, c)
    for c in range(H):
        forward(2, c)
    mate_copy.wait_recv()
    send_near(earlier)
    imgs[ROWS : 2 * ROWS] = unit_half(mate_raw[...])
    for c in range(H, C):
        forward(2, c)
    own_step()
    forward(3, 0)
    ring_step(1)
    forward(3, 1)
    ring_step(2)
    for c in range(H, C):
        forward(3, c)
    ring_step(3)

    sums_l = {}
    sums_r = {}

    def give_l(k, c, value):
        out_l[k - 1, chunk(c)] = value.astype(BF16)
        sums_l[k - 1, c] = send(out_l.at[k - 1, chunk(c)], in_l.at[k - 1, chunk(c)], back)

    def give_r(k, c, value):
        out_r[k - 1, chunk(c)] = value.astype(BF16)
        sums_r[k - 1, c] = send(out_r.at[k - 1, chunk(c)], in_r.at[k - 1, chunk(c)], fore)

    for c in range(H, C):
        d = C - 1 - c
        give_l(3, c, part[2, chunk(c)])
        give_r(3, d, part[2, upper(d)])

    answers = 3 + len(near) - greeted

    @pl.when(answers > 0)
    def _():
        pl.semaphore_wait(ready, answers)

    send_near([jnp.logical_not(known) for known in earlier])

    for c in range(H):
        gather_f[4, c].wait_recv()
        gather_b[4, C - 1 - c].wait_recv()
    texts = unit_half(far[...])
    pair = imgs[...]
    coef = negative(score(pair, texts))
    part_far[...] = dot_nn(coef.T, pair)
    for c in range(H):
        d = C - 1 - c
        give_l(4, c, part_far[chunk(c)])
        give_r(4, d, part_far[chunk(d)])
    img_acc[...] += dot_nn(coef, texts)
    img_out[...] = img_acc[ROWS : 2 * ROWS].astype(BF16)
    img_back = send(img_out, img_in, mate)

    def relay(k, c):
        d = C - 1 - c
        sums_l[k, c].wait_recv()
        give_l(k, c, part[k - 1, chunk(c)] + in_l[k, chunk(c)].astype(F32))
        sums_r[k, d].wait_recv()
        give_r(k, d, part[k - 1, upper(d)] + in_r[k, chunk(d)].astype(F32))

    for c in range(H, C):
        relay(2, c)
    for c in range(H):
        relay(3, c)
    for c in range(H, C):
        relay(1, c)
    for c in range(H):
        relay(2, c)

    for copy in near_copies:
        copy.wait_recv()
    texts = near_txt[...]
    coef = negative(score(imgs[0:ROWS], texts))
    img_acc[0:ROWS] += dot_nn(coef, texts)

    for c in range(H):
        relay(1, c)

    others = near_img[...]
    coef = negative(score(own_txt[...], others))
    txt_acc[...] += dot_nn(coef, others)
    img_back.wait_recv()
    gi_ref[...] = back_rows(
        img_v[...], norms[0], img_acc[0:ROWS] + img_in[...].astype(F32)
    )

    for c in range(H, C):
        d = C - 1 - c
        sums_l[0, c].wait_recv()
        sums_r[0, d].wait_recv()
        txt_acc[chunk(c)] += in_l[0, chunk(c)].astype(F32)
        txt_acc[chunk(d)] += in_r[0, chunk(d)].astype(F32)
    for c in range(H):
        d = C - 1 - c
        sums_l[0, c].wait_recv()
        gt_ref[chunk(c)] = back_rows(
            txt_v[chunk(c)],
            norms[1, chunk(c)],
            txt_acc[chunk(c)] + in_l[0, chunk(c)].astype(F32),
        )
        sums_r[0, d].wait_recv()
        gt_ref[chunk(d)] = back_rows(
            txt_v[chunk(d)],
            norms[1, chunk(d)],
            txt_acc[chunk(d)] + in_r[0, chunk(d)].astype(F32),
        )
    for copy in pending:
        copy.wait_send()


def store(gi_ref, gt_ref, oi_ref, ot_ref, sems):
    copies = [
        pltpu.make_async_copy(gi_ref, oi_ref, sems.at[0]),
        pltpu.make_async_copy(gt_ref, ot_ref, sems.at[1]),
    ]
    for copy in copies:
        copy.start()
    for copy in copies:
        copy.wait()


def per_device(images, texts, log_temp, bias):
    vmem = pl.BlockSpec(memory_space=pltpu.VMEM)
    hbm = pl.BlockSpec(memory_space=pltpu.HBM)
    out = jax.ShapeDtypeStruct((ROWS, D), F32)
    sums = pl.pallas_call(
        kernel,
        out_shape=(out, out),
        in_specs=[vmem] * 2 + [hbm] * 2,
        out_specs=(vmem, vmem),
        scratch_shapes=[
            pltpu.VMEM((ROWS, D), BF16),
            pltpu.VMEM((ROWS, D), BF16),
            pltpu.VMEM((ROWS, D), BF16),
            pltpu.VMEM((ROWS, D), BF16),
            pltpu.VMEM((2 * ROWS, D), BF16),
            pltpu.VMEM((3, 2 * ROWS, D), BF16),
            pltpu.VMEM((2 * ROWS, D), BF16),
            pltpu.VMEM((ROWS, D), BF16),
            pltpu.VMEM((4 * ROWS, D), BF16),
            pltpu.VMEM((4 * ROWS, D), BF16),
            pltpu.VMEM((2 * ROWS, D), F32),
            pltpu.VMEM((ROWS, D), F32),
            pltpu.VMEM((3, 2 * ROWS, D), F32),
            pltpu.VMEM((ROWS, D), F32),
            pltpu.VMEM((4, ROWS, D), BF16),
            pltpu.VMEM((4, ROWS, D), BF16),
            pltpu.VMEM((4, ROWS, D), BF16),
            pltpu.VMEM((4, ROWS, D), BF16),
            pltpu.VMEM((ROWS, D), BF16),
            pltpu.VMEM((ROWS, D), BF16),
            pltpu.VMEM((2, ROWS, 1), F32),
            pltpu.SemaphoreType.DMA((4,)),
            pltpu.SemaphoreType.DMA((2, 14 * C + 10)),
            pltpu.SemaphoreType.REGULAR,
        ],
        compiler_params=pltpu.CompilerParams(
            collective_id=0, has_side_effects=True, vmem_limit_bytes=40 * 1024 * 1024
        ),
        cost_estimate=pl.CostEstimate(
            flops=2_600_000_000, bytes_accessed=2_000_000, transcendentals=500_000
        ),
        name="pairs",
    )(
        log_temp.reshape(1, 1),
        bias.reshape(1, 1),
        pltpu.with_memory_space_constraint(images, pltpu.HBM),
        pltpu.with_memory_space_constraint(texts, pltpu.HBM),
    )
    return pl.pallas_call(
        store,
        out_shape=(out, out),
        in_specs=[vmem, vmem],
        out_specs=(hbm, hbm),
        scratch_shapes=[pltpu.SemaphoreType.DMA((2,))],
        compiler_params=pltpu.CompilerParams(vmem_limit_bytes=2 * 1024 * 1024),
        name="store",
    )(*sums)


def solution(mesh):
    return jax.shard_map(
        per_device,
        mesh=mesh,
        in_specs=(P(("grp", "blk"), None), P(("grp", "blk"), None), P(), P()),
        out_specs=(P(("grp", "blk"), None), P(("grp", "blk"), None)),
        check_vma=False,
    )
```

```python
import jax
import jax.numpy as jnp
from jax import lax
from jax.experimental import pallas as pl
from jax.experimental.pallas import tpu as pltpu
from jax.sharding import PartitionSpec as P

MESH = pl.DeviceIdType.MESH
ROWS = 128
D = 1152
RING = 8
C = 4
H = C // 2
R = ROWS // C
OFFSETS = (1, -1, 2, -2)

F32 = jnp.float32
BF16 = jnp.bfloat16


def dot_nt(a, b):
    return lax.dot_general(a, b, (((1,), (1,)), ((), ())), preferred_element_type=F32)


def dot_nn(a, b):
    return jnp.dot(a, b, preferred_element_type=F32)


def rows_norm(values):
    wide = values.astype(F32)
    return jnp.sqrt(jnp.sum(wide * wide, axis=1, keepdims=True) + 1e-06)


def unit_half(values):
    return (values.astype(F32) * (1.0 / rows_norm(values))).astype(BF16)


def back_rows(values, norms, upstream):
    rcp = 1.0 / norms
    unit = values.astype(F32) * rcp
    inner = jnp.sum(unit * upstream, axis=1, keepdims=True)
    return (upstream - unit * inner) * rcp


def rank_block(b):
    return jnp.where((b // 2) % 8 == 0, 0, 1000) + (b % 2) * 100 + b


def rank_ring(y):
    return jnp.where(y < RING // 2, y, RING + 3 - y)


def chunk(c):
    return pl.ds(c * R, R)


def kernel(
    temp_ref,
    bias_ref,
    img_ref,
    txt_ref,
    gi_ref,
    gt_ref,
    img_v,
    txt_v,
    own_txt,
    mate_raw,
    imgs,
    ring,
    ring_half,
    far,
    near_img,
    near_txt,
    img_acc,
    txt_acc,
    part,
    part_far,
    out_l,
    out_r,
    in_l,
    in_r,
    img_out,
    img_in,
    norms,
    local_sems,
    sems,
    ready,
):
    g = lax.axis_index("grp")
    b = lax.axis_index("blk")
    n_grp = lax.axis_size("grp")
    n_blk = lax.axis_size("blk")
    fore = ((g + 2) % n_grp, b)
    back = ((g + n_grp - 2) % n_grp, b)
    mate = (g + 1 - 2 * (g % 2), b)
    near_blk = [(b + n_blk + o) % n_blk for o in OFFSETS]
    near = [(g, n) for n in near_blk]
    y_rank = rank_ring(g // 2)
    fore_known = rank_ring(fore[0] // 2) < y_rank
    back_known = rank_ring(back[0] // 2) < y_rank
    mate_known = g % 2 == 1
    earlier = [rank_block(n) < rank_block(b) for n in near_blk]

    loads = []
    for i, (src, dst) in enumerate(((txt_ref, txt_v), (img_ref, img_v))):
        load = pltpu.make_async_copy(src, dst, local_sems.at[i])
        load.start()
        loads.append(load)

    partners = [(fore, fore_known, 1), (back, back_known, 0), (mate, mate_known, 2)]
    partners += [(dev, known, 3) for dev, known in zip(near, earlier)]
    barrier = pltpu.get_barrier_semaphore()
    greeted = 0
    for dev, known, _ in partners:

        @pl.when(jnp.logical_not(known))
        def _():
            pl.semaphore_signal(barrier, inc=1, device_id=dev, device_id_type=MESH)

        greeted = greeted + known.astype(jnp.int32)

    @pl.when(greeted > 0)
    def _():
        pl.semaphore_wait(barrier, greeted)

    for dev, known, place in partners:

        @pl.when(known)
        def _():
            pl.semaphore_signal(ready.at[place], inc=1, device_id=dev, device_id_type=MESH)

    pending = []
    count = [0]

    def prepare(src, dst, dev):
        i = count[0]
        count[0] += 1
        copy = pltpu.make_async_remote_copy(
            src_ref=src,
            dst_ref=dst,
            send_sem=sems.at[0, i],
            recv_sem=sems.at[1, i],
            device_id=dev,
            device_id_type=MESH,
        )
        pending.append(copy)
        return copy

    def send(src, dst, dev):
        copy = prepare(src, dst, dev)
        copy.start()
        return copy

    def upper(c):
        return pl.ds(ROWS + c * R, R)

    gather_f = {}
    gather_b = {}
    for c in range(C):
        gather_f[1, c] = prepare(txt_ref.at[chunk(c)], ring.at[0, chunk(c)], fore)
    for c in reversed(range(C)):
        gather_b[1, c] = prepare(txt_ref.at[chunk(c)], ring.at[0, upper(c)], back)
    mate_copy = prepare(img_ref, mate_raw, mate)
    first = [
        (list(gather_f[1, c] for c in range(C)), fore_known, 0),
        (list(gather_b[1, c] for c in reversed(range(C))), back_known, 1),
        ([mate_copy], mate_known, 2),
    ]
    for copies, known, _ in first:

        @pl.when(known)
        def _():
            for copy in copies:
                copy.start()

    for copies, known, place in first:

        @pl.when(jnp.logical_not(known))
        def _():
            pl.semaphore_wait(ready.at[place], 1)
            for copy in copies:
                copy.start()

    for load in loads:
        load.wait()
    norms[1] = rows_norm(txt_v[...])
    own_txt[...] = (txt_v[...].astype(F32) * (1.0 / norms[1])).astype(BF16)
    norms[0] = rows_norm(img_v[...])
    imgs[0:ROWS] = (img_v[...].astype(F32) * (1.0 / norms[0])).astype(BF16)
    scale = jnp.exp(temp_ref[...])
    offset = bias_ref[...]

    near_copies = []
    for i, dev in enumerate(near):
        rows = pl.ds(i * ROWS, ROWS)
        near_copies.append(prepare(imgs.at[pl.ds(0, ROWS)], near_img.at[rows], dev))
        near_copies.append(prepare(own_txt, near_txt.at[rows], dev))

    def send_near(which):
        for i in range(len(OFFSETS)):

            @pl.when(which[i])
            def _():
                near_copies[2 * i].start()
                near_copies[2 * i + 1].start()

    def forward(k, c):
        d = C - 1 - c
        gather_f[k, c].wait_recv()
        if k < 3:
            gather_f[k + 1, c] = send(ring.at[k - 1, chunk(c)], ring.at[k, chunk(c)], fore)
        elif c < H:
            gather_f[4, c] = send(ring.at[k - 1, chunk(c)], far.at[chunk(c)], fore)
        gather_b[k, d].wait_recv()
        if k < 3:
            gather_b[k + 1, d] = send(ring.at[k - 1, upper(d)], ring.at[k, upper(d)], back)
        elif d >= H:
            gather_b[4, d] = send(ring.at[k - 1, upper(d)], far.at[chunk(d)], back)

    def negative(logits):
        return (jax.nn.sigmoid(logits) * scale).astype(BF16)

    def score(a, c):
        return scale * dot_nt(a, c) + offset

    def ring_step(k):
        ring_half[...] = unit_half(ring[k - 1])
        texts = ring_half[...]
        pair = imgs[...]
        coef = negative(score(pair, texts))
        part[k - 1] = dot_nn(coef.T, pair)
        img_acc[...] += dot_nn(coef, texts)

    def own_step():
        texts = own_txt[...]
        pair = imgs[...]
        logits = score(pair, texts)
        same = lax.broadcasted_iota(jnp.int32, logits.shape, 0) == lax.broadcasted_iota(
            jnp.int32, logits.shape, 1
        )
        sign = jnp.where(same, jnp.float32(1.0), jnp.float32(-1.0))
        coef = (-sign * jax.nn.sigmoid(-sign * logits) * scale).astype(BF16)
        img_acc[...] = dot_nn(coef, texts)
        txt_acc[...] = dot_nn(coef.T, pair)

    for c in range(C):
        forward(1, c)
    for c in range(H):
        forward(2, c)
    mate_copy.wait_recv()
    send_near(earlier)
    imgs[ROWS : 2 * ROWS] = unit_half(mate_raw[...])
    for c in range(H, C):
        forward(2, c)
    own_step()
    for c in range(H // 2):
        forward(3, c)
    ring_step(1)
    answers = len(near) - sum(known.astype(jnp.int32) for known in earlier)

    @pl.when(answers > 0)
    def _():
        pl.semaphore_wait(ready.at[3], answers)

    send_near([jnp.logical_not(known) for known in earlier])
    for c in range(H // 2, H):
        forward(3, c)
    ring_step(2)
    for c in range(H, C):
        forward(3, c)
    ring_step(3)

    sums_l = {}
    sums_r = {}

    def give_l(k, c, value):
        out_l[k - 1, chunk(c)] = value.astype(BF16)
        sums_l[k - 1, c] = send(out_l.at[k - 1, chunk(c)], in_l.at[k - 1, chunk(c)], back)

    def give_r(k, c, value):
        out_r[k - 1, chunk(c)] = value.astype(BF16)
        sums_r[k - 1, c] = send(out_r.at[k - 1, chunk(c)], in_r.at[k - 1, chunk(c)], fore)

    for c in range(H, C):
        d = C - 1 - c
        give_l(3, c, part[2, chunk(c)])
        give_r(3, d, part[2, upper(d)])

    for c in range(H):
        gather_f[4, c].wait_recv()
        gather_b[4, C - 1 - c].wait_recv()
    texts = unit_half(far[...])
    pair = imgs[...]
    coef = negative(score(pair, texts))
    part_far[...] = dot_nn(coef.T, pair)
    for c in range(H):
        d = C - 1 - c
        give_l(4, c, part_far[chunk(c)])
        give_r(4, d, part_far[chunk(d)])
    img_acc[...] += dot_nn(coef, texts)
    img_out[...] = img_acc[ROWS : 2 * ROWS].astype(BF16)
    img_back = send(img_out, img_in, mate)

    def relay(k, c):
        d = C - 1 - c
        sums_l[k, c].wait_recv()
        give_l(k, c, part[k - 1, chunk(c)] + in_l[k, chunk(c)].astype(F32))
        sums_r[k, d].wait_recv()
        give_r(k, d, part[k - 1, upper(d)] + in_r[k, chunk(d)].astype(F32))

    for c in range(H, C):
        relay(2, c)
    for c in range(H):
        relay(3, c)
    for c in range(H, C):
        relay(1, c)
    for c in range(H):
        relay(2, c)

    for c in range(H):
        relay(1, c)

    for copy in near_copies:
        copy.wait_recv()
    texts = near_txt[...]
    coef = negative(score(imgs[0:ROWS], texts))
    img_acc[0:ROWS] += dot_nn(coef, texts)

    others = near_img[...]
    coef = negative(score(own_txt[...], others))
    txt_acc[...] += dot_nn(coef, others)
    img_back.wait_recv()
    gi_ref[...] = back_rows(
        img_v[...], norms[0], img_acc[0:ROWS] + img_in[...].astype(F32)
    )

    for c in range(H, C):
        d = C - 1 - c
        sums_l[0, c].wait_recv()
        sums_r[0, d].wait_recv()
        txt_acc[chunk(c)] += in_l[0, chunk(c)].astype(F32)
        txt_acc[chunk(d)] += in_r[0, chunk(d)].astype(F32)
    for c in range(H):
        d = C - 1 - c
        sums_l[0, c].wait_recv()
        gt_ref[chunk(c)] = back_rows(
            txt_v[chunk(c)],
            norms[1, chunk(c)],
            txt_acc[chunk(c)] + in_l[0, chunk(c)].astype(F32),
        )
        sums_r[0, d].wait_recv()
        gt_ref[chunk(d)] = back_rows(
            txt_v[chunk(d)],
            norms[1, chunk(d)],
            txt_acc[chunk(d)] + in_r[0, chunk(d)].astype(F32),
        )
    for copy in pending:
        copy.wait_send()


def store(gi_ref, gt_ref, oi_ref, ot_ref, sems):
    copies = [
        pltpu.make_async_copy(gi_ref, oi_ref, sems.at[0]),
        pltpu.make_async_copy(gt_ref, ot_ref, sems.at[1]),
    ]
    for copy in copies:
        copy.start()
    for copy in copies:
        copy.wait()


def per_device(images, texts, log_temp, bias):
    vmem = pl.BlockSpec(memory_space=pltpu.VMEM)
    hbm = pl.BlockSpec(memory_space=pltpu.HBM)
    out = jax.ShapeDtypeStruct((ROWS, D), F32)
    sums = pl.pallas_call(
        kernel,
        out_shape=(out, out),
        in_specs=[vmem] * 2 + [hbm] * 2,
        out_specs=(vmem, vmem),
        scratch_shapes=[
            pltpu.VMEM((ROWS, D), BF16),
            pltpu.VMEM((ROWS, D), BF16),
            pltpu.VMEM((ROWS, D), BF16),
            pltpu.VMEM((ROWS, D), BF16),
            pltpu.VMEM((2 * ROWS, D), BF16),
            pltpu.VMEM((3, 2 * ROWS, D), BF16),
            pltpu.VMEM((2 * ROWS, D), BF16),
            pltpu.VMEM((ROWS, D), BF16),
            pltpu.VMEM((4 * ROWS, D), BF16),
            pltpu.VMEM((4 * ROWS, D), BF16),
            pltpu.VMEM((2 * ROWS, D), F32),
            pltpu.VMEM((ROWS, D), F32),
            pltpu.VMEM((3, 2 * ROWS, D), F32),
            pltpu.VMEM((ROWS, D), F32),
            pltpu.VMEM((4, ROWS, D), BF16),
            pltpu.VMEM((4, ROWS, D), BF16),
            pltpu.VMEM((4, ROWS, D), BF16),
            pltpu.VMEM((4, ROWS, D), BF16),
            pltpu.VMEM((ROWS, D), BF16),
            pltpu.VMEM((ROWS, D), BF16),
            pltpu.VMEM((2, ROWS, 1), F32),
            pltpu.SemaphoreType.DMA((4,)),
            pltpu.SemaphoreType.DMA((2, 14 * C + 10)),
            pltpu.SemaphoreType.REGULAR((4,)),
        ],
        compiler_params=pltpu.CompilerParams(
            collective_id=0, has_side_effects=True, vmem_limit_bytes=40 * 1024 * 1024
        ),
        cost_estimate=pl.CostEstimate(
            flops=2_600_000_000, bytes_accessed=2_000_000, transcendentals=500_000
        ),
        name="pairs",
    )(
        log_temp.reshape(1, 1),
        bias.reshape(1, 1),
        pltpu.with_memory_space_constraint(images, pltpu.HBM),
        pltpu.with_memory_space_constraint(texts, pltpu.HBM),
    )
    return pl.pallas_call(
        store,
        out_shape=(out, out),
        in_specs=[vmem, vmem],
        out_specs=(hbm, hbm),
        scratch_shapes=[pltpu.SemaphoreType.DMA((2,))],
        compiler_params=pltpu.CompilerParams(vmem_limit_bytes=2 * 1024 * 1024),
        name="store",
    )(*sums)


def solution(mesh):
    return jax.shard_map(
        per_device,
        mesh=mesh,
        in_specs=(P(("grp", "blk"), None), P(("grp", "blk"), None), P(), P()),
        out_specs=(P(("grp", "blk"), None), P(("grp", "blk"), None)),
        check_vma=False,
    )
```

```python
import jax
import jax.numpy as jnp
from jax import lax
from jax.experimental import pallas as pl
from jax.experimental.pallas import tpu as pltpu
from jax.sharding import PartitionSpec as P

MESH = pl.DeviceIdType.MESH
ROWS = 128
D = 1152
RING = 8
C = 4
H = C // 2
R = ROWS // C
OFFSETS = (1, -1, 2, -2)

F32 = jnp.float32
BF16 = jnp.bfloat16


def dot_nt(a, b):
    return lax.dot_general(a, b, (((1,), (1,)), ((), ())), preferred_element_type=F32)


def dot_nn(a, b):
    return jnp.dot(a, b, preferred_element_type=F32)


def rows_norm(values):
    wide = values.astype(F32)
    return jnp.sqrt(jnp.sum(wide * wide, axis=1, keepdims=True) + 1e-06)


def unit_half(values):
    return (values.astype(F32) * (1.0 / rows_norm(values))).astype(BF16)


def back_rows(values, norms, upstream):
    rcp = 1.0 / norms
    unit = values.astype(F32) * rcp
    inner = jnp.sum(unit * upstream, axis=1, keepdims=True)
    return (upstream - unit * inner) * rcp


def rank_block(b):
    return jnp.where((b // 2) % 8 == 0, 0, 1000) + (b % 2) * 100 + b


def rank_ring(y):
    return jnp.where(y < RING // 2, y, RING + 3 - y)


def chunk(c):
    return pl.ds(c * R, R)


def kernel(
    temp_ref,
    bias_ref,
    img_ref,
    txt_ref,
    gi_ref,
    gt_ref,
    img_v,
    txt_v,
    own_txt,
    mate_raw,
    imgs,
    ring,
    ring_half,
    far,
    near_img,
    near_txt,
    img_acc,
    txt_acc,
    part,
    part_far,
    out_l,
    out_r,
    in_l,
    in_r,
    img_out,
    img_in,
    norms,
    local_sems,
    sems,
    ready,
):
    g = lax.axis_index("grp")
    b = lax.axis_index("blk")
    n_grp = lax.axis_size("grp")
    n_blk = lax.axis_size("blk")
    fore = ((g + 2) % n_grp, b)
    back = ((g + n_grp - 2) % n_grp, b)
    mate = (g + 1 - 2 * (g % 2), b)
    near_blk = [(b + n_blk + o) % n_blk for o in OFFSETS]
    near = [(g, n) for n in near_blk]
    y_rank = rank_ring(g // 2)
    fore_known = rank_ring(fore[0] // 2) < y_rank
    back_known = rank_ring(back[0] // 2) < y_rank
    mate_known = g % 2 == 1
    earlier = [rank_block(n) < rank_block(b) for n in near_blk]

    loads = []
    for i, (src, dst) in enumerate(((txt_ref, txt_v), (img_ref, img_v))):
        load = pltpu.make_async_copy(src, dst, local_sems.at[i])
        load.start()
        loads.append(load)

    partners = [(fore, fore_known, 1), (back, back_known, 0), (mate, mate_known, 2)]
    partners += [(dev, known, 3) for dev, known in zip(near, earlier)]
    barrier = pltpu.get_barrier_semaphore()
    greeted = 0
    for dev, known, _ in partners:

        @pl.when(jnp.logical_not(known))
        def _():
            pl.semaphore_signal(barrier, inc=1, device_id=dev, device_id_type=MESH)

        greeted = greeted + known.astype(jnp.int32)

    @pl.when(greeted > 0)
    def _():
        pl.semaphore_wait(barrier, greeted)

    for dev, known, place in partners:

        @pl.when(known)
        def _():
            pl.semaphore_signal(ready.at[place], inc=1, device_id=dev, device_id_type=MESH)

    pending = []
    count = [0]

    def prepare(src, dst, dev):
        i = count[0]
        count[0] += 1
        copy = pltpu.make_async_remote_copy(
            src_ref=src,
            dst_ref=dst,
            send_sem=sems.at[0, i],
            recv_sem=sems.at[1, i],
            device_id=dev,
            device_id_type=MESH,
        )
        pending.append(copy)
        return copy

    def send(src, dst, dev):
        copy = prepare(src, dst, dev)
        copy.start()
        return copy

    def upper(c):
        return pl.ds(ROWS + c * R, R)

    gather_f = {}
    gather_b = {}
    for c in range(C):
        gather_f[1, c] = prepare(txt_ref.at[chunk(c)], ring.at[0, chunk(c)], fore)
    for c in reversed(range(C)):
        gather_b[1, c] = prepare(txt_ref.at[chunk(c)], ring.at[0, upper(c)], back)
    mate_copy = prepare(img_ref, mate_raw, mate)
    first = [
        (list(gather_f[1, c] for c in range(C)), fore_known, 0),
        (list(gather_b[1, c] for c in reversed(range(C))), back_known, 1),
        ([mate_copy], mate_known, 2),
    ]
    for copies, known, _ in first:

        @pl.when(known)
        def _():
            for copy in copies:
                copy.start()

    for copies, known, place in first:

        @pl.when(jnp.logical_not(known))
        def _():
            pl.semaphore_wait(ready.at[place], 1)
            for copy in copies:
                copy.start()

    for load in loads:
        load.wait()
    norms[1] = rows_norm(txt_v[...])
    own_txt[...] = (txt_v[...].astype(F32) * (1.0 / norms[1])).astype(BF16)
    norms[0] = rows_norm(img_v[...])
    imgs[0:ROWS] = (img_v[...].astype(F32) * (1.0 / norms[0])).astype(BF16)
    scale = jnp.exp(temp_ref[...])
    offset = bias_ref[...]

    near_copies = []
    for i, dev in enumerate(near):
        rows = pl.ds(i * ROWS, ROWS)
        near_copies.append(prepare(imgs.at[pl.ds(0, ROWS)], near_img.at[rows], dev))
        near_copies.append(prepare(own_txt, near_txt.at[rows], dev))

    def send_near(which):
        for i in range(len(OFFSETS)):

            @pl.when(which[i])
            def _():
                near_copies[2 * i].start()
                near_copies[2 * i + 1].start()

    def forward(k, c):
        d = C - 1 - c
        gather_f[k, c].wait_recv()
        if k < 3:
            gather_f[k + 1, c] = send(ring.at[k - 1, chunk(c)], ring.at[k, chunk(c)], fore)
        elif c < H:
            gather_f[4, c] = send(ring.at[k - 1, chunk(c)], far.at[chunk(c)], fore)
        gather_b[k, d].wait_recv()
        if k < 3:
            gather_b[k + 1, d] = send(ring.at[k - 1, upper(d)], ring.at[k, upper(d)], back)
        elif d >= H:
            gather_b[4, d] = send(ring.at[k - 1, upper(d)], far.at[chunk(d)], back)

    def negative(logits):
        return (jax.nn.sigmoid(logits) * scale).astype(BF16)

    def score(a, c):
        return scale * dot_nt(a, c) + offset

    def ring_step(k):
        ring_half[...] = unit_half(ring[k - 1])
        texts = ring_half[...]
        pair = imgs[...]
        coef = negative(score(pair, texts))
        part[k - 1] = dot_nn(coef.T, pair)
        img_acc[...] += dot_nn(coef, texts)

    def own_step():
        texts = own_txt[...]
        pair = imgs[...]
        logits = score(pair, texts)
        same = lax.broadcasted_iota(jnp.int32, logits.shape, 0) == lax.broadcasted_iota(
            jnp.int32, logits.shape, 1
        )
        sign = jnp.where(same, jnp.float32(1.0), jnp.float32(-1.0))
        coef = (-sign * jax.nn.sigmoid(-sign * logits) * scale).astype(BF16)
        img_acc[...] = dot_nn(coef, texts)
        txt_acc[...] = dot_nn(coef.T, pair)

    for c in range(C):
        forward(1, c)
    for c in range(H):
        forward(2, c)
    mate_copy.wait_recv()
    send_near(earlier)
    imgs[ROWS : 2 * ROWS] = unit_half(mate_raw[...])
    for c in range(H, C):
        forward(2, c)
    own_step()
    for c in range(H // 2):
        forward(3, c)
    ring_step(1)
    answers = len(near) - sum(known.astype(jnp.int32) for known in earlier)

    @pl.when(answers > 0)
    def _():
        pl.semaphore_wait(ready.at[3], answers)

    send_near([jnp.logical_not(known) for known in earlier])
    for c in range(H // 2, H):
        forward(3, c)
    ring_step(2)
    for c in range(H, C):
        forward(3, c)
    ring_step(3)

    sums_l = {}
    sums_r = {}

    def give_l(k, c, value):
        out_l[k - 1, chunk(c)] = value.astype(BF16)
        sums_l[k - 1, c] = send(out_l.at[k - 1, chunk(c)], in_l.at[k - 1, chunk(c)], back)

    def give_r(k, c, value):
        out_r[k - 1, chunk(c)] = value.astype(BF16)
        sums_r[k - 1, c] = send(out_r.at[k - 1, chunk(c)], in_r.at[k - 1, chunk(c)], fore)

    for c in range(H, C):
        d = C - 1 - c
        give_l(3, c, part[2, chunk(c)])
        give_r(3, d, part[2, upper(d)])

    for c in range(H):
        gather_f[4, c].wait_recv()
        gather_b[4, C - 1 - c].wait_recv()
    texts = unit_half(far[...])
    pair = imgs[...]
    coef = negative(score(pair, texts))
    part_far[...] = dot_nn(coef.T, pair)
    for c in range(H):
        d = C - 1 - c
        give_l(4, c, part_far[chunk(c)])
        give_r(4, d, part_far[chunk(d)])
    img_acc[...] += dot_nn(coef, texts)
    img_out[...] = img_acc[ROWS : 2 * ROWS].astype(BF16)
    img_back = send(img_out, img_in, mate)

    def relay(k, c):
        d = C - 1 - c
        sums_l[k, c].wait_recv()
        give_l(k, c, part[k - 1, chunk(c)] + in_l[k, chunk(c)].astype(F32))
        sums_r[k, d].wait_recv()
        give_r(k, d, part[k - 1, upper(d)] + in_r[k, chunk(d)].astype(F32))

    for c in range(H):
        relay(3, c)
    for c in range(H, C):
        relay(2, c)
    for c in range(H):
        relay(2, c)
    for c in range(H, C):
        relay(1, c)

    for c in range(H):
        relay(1, c)

    recent = 4 * H
    for copy in pending[:-recent]:
        copy.wait_send()

    for copy in near_copies:
        copy.wait_recv()
    texts = near_txt[...]
    coef = negative(score(imgs[0:ROWS], texts))
    img_acc[0:ROWS] += dot_nn(coef, texts)

    others = near_img[...]
    coef = negative(score(own_txt[...], others))
    txt_acc[...] += dot_nn(coef, others)
    img_back.wait_recv()
    gi_ref[...] = back_rows(
        img_v[...], norms[0], img_acc[0:ROWS] + img_in[...].astype(F32)
    )

    for c in range(H, C):
        d = C - 1 - c
        sums_l[0, c].wait_recv()
        sums_r[0, d].wait_recv()
        txt_acc[chunk(c)] += in_l[0, chunk(c)].astype(F32)
        txt_acc[chunk(d)] += in_r[0, chunk(d)].astype(F32)
    for c in range(H):
        d = C - 1 - c
        sums_l[0, c].wait_recv()
        gt_ref[chunk(c)] = back_rows(
            txt_v[chunk(c)],
            norms[1, chunk(c)],
            txt_acc[chunk(c)] + in_l[0, chunk(c)].astype(F32),
        )
        sums_r[0, d].wait_recv()
        gt_ref[chunk(d)] = back_rows(
            txt_v[chunk(d)],
            norms[1, chunk(d)],
            txt_acc[chunk(d)] + in_r[0, chunk(d)].astype(F32),
        )
    for copy in pending[-recent:]:
        copy.wait_send()


def store(gi_ref, gt_ref, oi_ref, ot_ref, sems):
    copies = [
        pltpu.make_async_copy(gi_ref, oi_ref, sems.at[0]),
        pltpu.make_async_copy(gt_ref, ot_ref, sems.at[1]),
    ]
    for copy in copies:
        copy.start()
    for copy in copies:
        copy.wait()


def per_device(images, texts, log_temp, bias):
    vmem = pl.BlockSpec(memory_space=pltpu.VMEM)
    hbm = pl.BlockSpec(memory_space=pltpu.HBM)
    out = jax.ShapeDtypeStruct((ROWS, D), F32)
    sums = pl.pallas_call(
        kernel,
        out_shape=(out, out),
        in_specs=[vmem] * 2 + [hbm] * 2,
        out_specs=(vmem, vmem),
        scratch_shapes=[
            pltpu.VMEM((ROWS, D), BF16),
            pltpu.VMEM((ROWS, D), BF16),
            pltpu.VMEM((ROWS, D), BF16),
            pltpu.VMEM((ROWS, D), BF16),
            pltpu.VMEM((2 * ROWS, D), BF16),
            pltpu.VMEM((3, 2 * ROWS, D), BF16),
            pltpu.VMEM((2 * ROWS, D), BF16),
            pltpu.VMEM((ROWS, D), BF16),
            pltpu.VMEM((4 * ROWS, D), BF16),
            pltpu.VMEM((4 * ROWS, D), BF16),
            pltpu.VMEM((2 * ROWS, D), F32),
            pltpu.VMEM((ROWS, D), F32),
            pltpu.VMEM((3, 2 * ROWS, D), F32),
            pltpu.VMEM((ROWS, D), F32),
            pltpu.VMEM((4, ROWS, D), BF16),
            pltpu.VMEM((4, ROWS, D), BF16),
            pltpu.VMEM((4, ROWS, D), BF16),
            pltpu.VMEM((4, ROWS, D), BF16),
            pltpu.VMEM((ROWS, D), BF16),
            pltpu.VMEM((ROWS, D), BF16),
            pltpu.VMEM((2, ROWS, 1), F32),
            pltpu.SemaphoreType.DMA((4,)),
            pltpu.SemaphoreType.DMA((2, 14 * C + 10)),
            pltpu.SemaphoreType.REGULAR((4,)),
        ],
        compiler_params=pltpu.CompilerParams(
            collective_id=0, has_side_effects=True, vmem_limit_bytes=40 * 1024 * 1024
        ),
        cost_estimate=pl.CostEstimate(
            flops=2_600_000_000, bytes_accessed=2_000_000, transcendentals=500_000
        ),
        name="pairs",
    )(
        log_temp.reshape(1, 1),
        bias.reshape(1, 1),
        pltpu.with_memory_space_constraint(images, pltpu.HBM),
        pltpu.with_memory_space_constraint(texts, pltpu.HBM),
    )
    return pl.pallas_call(
        store,
        out_shape=(out, out),
        in_specs=[vmem, vmem],
        out_specs=(hbm, hbm),
        scratch_shapes=[pltpu.SemaphoreType.DMA((2,))],
        compiler_params=pltpu.CompilerParams(vmem_limit_bytes=2 * 1024 * 1024),
        name="store",
    )(*sums)


def solution(mesh):
    return jax.shard_map(
        per_device,
        mesh=mesh,
        in_specs=(P(("grp", "blk"), None), P(("grp", "blk"), None), P(), P()),
        out_specs=(P(("grp", "blk"), None), P(("grp", "blk"), None)),
        check_vma=False,
    )
```

```python
import jax
import jax.numpy as jnp
from jax import lax
from jax.experimental import pallas as pl
from jax.experimental.pallas import tpu as pltpu
from jax.sharding import PartitionSpec as P

MESH = pl.DeviceIdType.MESH
ROWS = 128
D = 1152
RING = 8
C = 4
H = C // 2
R = ROWS // C
OFFSETS = (1, -1, 2, -2)

F32 = jnp.float32
BF16 = jnp.bfloat16


def dot_nt(a, b):
    return lax.dot_general(a, b, (((1,), (1,)), ((), ())), preferred_element_type=F32)


def dot_nn(a, b):
    return jnp.dot(a, b, preferred_element_type=F32)


def rows_norm(values):
    wide = values.astype(F32)
    return jnp.sqrt(jnp.sum(wide * wide, axis=1, keepdims=True) + 1e-06)


def unit_half(values):
    return (values.astype(F32) * (1.0 / rows_norm(values))).astype(BF16)


def back_rows(values, norms, upstream):
    rcp = 1.0 / norms
    unit = values.astype(F32) * rcp
    inner = jnp.sum(unit * upstream, axis=1, keepdims=True)
    return (upstream - unit * inner) * rcp


def rank_block(b):
    return jnp.where((b // 2) % 8 == 0, 0, 1000) + (b % 2) * 100 + b


def rank_ring(y):
    return jnp.where(y < RING // 2, y, RING + 3 - y)


def chunk(c):
    return pl.ds(c * R, R)


def kernel(
    temp_ref,
    bias_ref,
    img_ref,
    txt_ref,
    gi_ref,
    gt_ref,
    img_v,
    txt_v,
    own_txt,
    mate_raw,
    imgs,
    ring,
    ring_half,
    far,
    near_img,
    near_txt,
    img_acc,
    txt_acc,
    part,
    part_far,
    out_l,
    out_r,
    in_l,
    in_r,
    img_out,
    img_in,
    norms,
    local_sems,
    sems,
    ready,
):
    g = lax.axis_index("grp")
    b = lax.axis_index("blk")
    n_grp = lax.axis_size("grp")
    n_blk = lax.axis_size("blk")
    fore = ((g + 2) % n_grp, b)
    back = ((g + n_grp - 2) % n_grp, b)
    mate = (g + 1 - 2 * (g % 2), b)
    near_blk = [(b + n_blk + o) % n_blk for o in OFFSETS]
    near = [(g, n) for n in near_blk]
    y_rank = rank_ring(g // 2)
    fore_known = rank_ring(fore[0] // 2) < y_rank
    back_known = rank_ring(back[0] // 2) < y_rank
    mate_known = g % 2 == 1
    earlier = [rank_block(n) < rank_block(b) for n in near_blk]

    loads = []
    for i, (src, dst) in enumerate(((txt_ref, txt_v), (img_ref, img_v))):
        load = pltpu.make_async_copy(src, dst, local_sems.at[i])
        load.start()
        loads.append(load)

    partners = [(fore, fore_known, 1), (back, back_known, 0), (mate, mate_known, 2)]
    partners += [(dev, known, 3) for dev, known in zip(near, earlier)]
    barrier = pltpu.get_barrier_semaphore()
    greeted = 0
    for dev, known, _ in partners:

        @pl.when(jnp.logical_not(known))
        def _():
            pl.semaphore_signal(barrier, inc=1, device_id=dev, device_id_type=MESH)

        greeted = greeted + known.astype(jnp.int32)

    @pl.when(greeted > 0)
    def _():
        pl.semaphore_wait(barrier, greeted)

    for dev, known, place in partners:

        @pl.when(known)
        def _():
            pl.semaphore_signal(ready.at[place], inc=1, device_id=dev, device_id_type=MESH)

    pending = []
    count = [0]

    def prepare(src, dst, dev):
        i = count[0]
        count[0] += 1
        copy = pltpu.make_async_remote_copy(
            src_ref=src,
            dst_ref=dst,
            send_sem=sems.at[0, i],
            recv_sem=sems.at[1, i],
            device_id=dev,
            device_id_type=MESH,
        )
        pending.append(copy)
        return copy

    def send(src, dst, dev):
        copy = prepare(src, dst, dev)
        copy.start()
        return copy

    def upper(c):
        return pl.ds(ROWS + c * R, R)

    gather_f = {}
    gather_b = {}
    for c in range(C):
        gather_f[1, c] = prepare(txt_ref.at[chunk(c)], ring.at[0, chunk(c)], fore)
    for c in reversed(range(C)):
        gather_b[1, c] = prepare(txt_ref.at[chunk(c)], ring.at[0, upper(c)], back)
    mate_copy = prepare(img_ref, mate_raw, mate)
    first = [
        (list(gather_f[1, c] for c in range(C)), fore_known, 0),
        (list(gather_b[1, c] for c in reversed(range(C))), back_known, 1),
        ([mate_copy], mate_known, 2),
    ]
    for copies, known, _ in first:

        @pl.when(known)
        def _():
            for copy in copies:
                copy.start()

    for copies, known, place in first:

        @pl.when(jnp.logical_not(known))
        def _():
            pl.semaphore_wait(ready.at[place], 1)
            for copy in copies:
                copy.start()

    for load in loads:
        load.wait()
    norms[1] = rows_norm(txt_v[...])
    own_txt[...] = (txt_v[...].astype(F32) * (1.0 / norms[1])).astype(BF16)
    norms[0] = rows_norm(img_v[...])
    imgs[0:ROWS] = (img_v[...].astype(F32) * (1.0 / norms[0])).astype(BF16)
    scale = jnp.exp(temp_ref[...])
    offset = bias_ref[...]

    near_copies = []
    for i, dev in enumerate(near):
        rows = pl.ds(i * ROWS, ROWS)
        near_copies.append(prepare(imgs.at[pl.ds(0, ROWS)], near_img.at[rows], dev))
        near_copies.append(prepare(own_txt, near_txt.at[rows], dev))

    def send_near(which):
        for i in range(len(OFFSETS)):

            @pl.when(which[i])
            def _():
                near_copies[2 * i].start()
                near_copies[2 * i + 1].start()

    def forward(k, c):
        d = C - 1 - c
        gather_f[k, c].wait_recv()
        if k < 3:
            gather_f[k + 1, c] = send(ring.at[k - 1, chunk(c)], ring.at[k, chunk(c)], fore)
        elif c < H:
            gather_f[4, c] = send(ring.at[k - 1, chunk(c)], far.at[chunk(c)], fore)
        gather_b[k, d].wait_recv()
        if k < 3:
            gather_b[k + 1, d] = send(ring.at[k - 1, upper(d)], ring.at[k, upper(d)], back)
        elif d >= H:
            gather_b[4, d] = send(ring.at[k - 1, upper(d)], far.at[chunk(d)], back)

    def negative(logits):
        return (jax.nn.sigmoid(logits) * scale).astype(BF16)

    def score(a, c):
        return scale * dot_nt(a, c) + offset

    def ring_step(k):
        ring_half[...] = unit_half(ring[k - 1])
        texts = ring_half[...]
        pair = imgs[...]
        coef = negative(score(pair, texts))
        part[k - 1] = dot_nn(coef.T, pair)
        img_acc[...] += dot_nn(coef, texts)

    def own_step():
        texts = own_txt[...]
        pair = imgs[...]
        logits = score(pair, texts)
        same = lax.broadcasted_iota(jnp.int32, logits.shape, 0) == lax.broadcasted_iota(
            jnp.int32, logits.shape, 1
        )
        sign = jnp.where(same, jnp.float32(1.0), jnp.float32(-1.0))
        coef = (-sign * jax.nn.sigmoid(-sign * logits) * scale).astype(BF16)
        img_acc[...] = dot_nn(coef, texts)
        txt_acc[...] = dot_nn(coef.T, pair)

    for c in range(C):
        forward(1, c)
    for c in range(H):
        forward(2, c)
    send_near(earlier)
    for c in range(H, C):
        forward(2, c)
    mate_copy.wait_recv()
    imgs[ROWS : 2 * ROWS] = unit_half(mate_raw[...])
    own_step()
    for c in range(H // 2):
        forward(3, c)
    ring_step(1)
    answers = len(near) - sum(known.astype(jnp.int32) for known in earlier)

    @pl.when(answers > 0)
    def _():
        pl.semaphore_wait(ready.at[3], answers)

    send_near([jnp.logical_not(known) for known in earlier])
    for c in range(H // 2, H):
        forward(3, c)
    ring_step(2)
    for c in range(H, C):
        forward(3, c)
    ring_step(3)

    sums_l = {}
    sums_r = {}

    def give_l(k, c, value):
        out_l[k - 1, chunk(c)] = value.astype(BF16)
        sums_l[k - 1, c] = send(out_l.at[k - 1, chunk(c)], in_l.at[k - 1, chunk(c)], back)

    def give_r(k, c, value):
        out_r[k - 1, chunk(c)] = value.astype(BF16)
        sums_r[k - 1, c] = send(out_r.at[k - 1, chunk(c)], in_r.at[k - 1, chunk(c)], fore)

    for c in range(H, C):
        d = C - 1 - c
        give_l(3, c, part[2, chunk(c)])
        give_r(3, d, part[2, upper(d)])

    for c in range(H):
        gather_f[4, c].wait_recv()
        gather_b[4, C - 1 - c].wait_recv()
    texts = unit_half(far[...])
    pair = imgs[...]
    coef = negative(score(pair, texts))
    part_far[...] = dot_nn(coef.T, pair)
    for c in range(H):
        d = C - 1 - c
        give_l(4, c, part_far[chunk(c)])
        give_r(4, d, part_far[chunk(d)])
    img_acc[...] += dot_nn(coef, texts)
    img_out[...] = img_acc[ROWS : 2 * ROWS].astype(BF16)
    img_back = send(img_out, img_in, mate)

    def relay(k, c):
        d = C - 1 - c
        sums_l[k, c].wait_recv()
        give_l(k, c, part[k - 1, chunk(c)] + in_l[k, chunk(c)].astype(F32))
        sums_r[k, d].wait_recv()
        give_r(k, d, part[k - 1, upper(d)] + in_r[k, chunk(d)].astype(F32))

    for c in range(H):
        relay(3, c)
    for c in range(H, C):
        relay(2, c)
    for c in range(H):
        relay(2, c)
    for c in range(H, C):
        relay(1, c)

    for c in range(H):
        relay(1, c)

    recent = 4 * H
    for copy in pending[:-recent]:
        copy.wait_send()

    for copy in near_copies:
        copy.wait_recv()
    texts = near_txt[...]
    coef = negative(score(imgs[0:ROWS], texts))
    img_acc[0:ROWS] += dot_nn(coef, texts)

    others = near_img[...]
    coef = negative(score(own_txt[...], others))
    txt_acc[...] += dot_nn(coef, others)
    img_back.wait_recv()
    gi_ref[...] = back_rows(
        img_v[...], norms[0], img_acc[0:ROWS] + img_in[...].astype(F32)
    )

    for c in range(H, C):
        d = C - 1 - c
        sums_l[0, c].wait_recv()
        sums_r[0, d].wait_recv()
        txt_acc[chunk(c)] += in_l[0, chunk(c)].astype(F32)
        txt_acc[chunk(d)] += in_r[0, chunk(d)].astype(F32)
    for c in range(H):
        d = C - 1 - c
        sums_l[0, c].wait_recv()
        gt_ref[chunk(c)] = back_rows(
            txt_v[chunk(c)],
            norms[1, chunk(c)],
            txt_acc[chunk(c)] + in_l[0, chunk(c)].astype(F32),
        )
        sums_r[0, d].wait_recv()
        gt_ref[chunk(d)] = back_rows(
            txt_v[chunk(d)],
            norms[1, chunk(d)],
            txt_acc[chunk(d)] + in_r[0, chunk(d)].astype(F32),
        )
    for copy in pending[-recent:]:
        copy.wait_send()


def store(gi_ref, gt_ref, oi_ref, ot_ref, sems):
    copies = [
        pltpu.make_async_copy(gi_ref, oi_ref, sems.at[0]),
        pltpu.make_async_copy(gt_ref, ot_ref, sems.at[1]),
    ]
    for copy in copies:
        copy.start()
    for copy in copies:
        copy.wait()


def per_device(images, texts, log_temp, bias):
    vmem = pl.BlockSpec(memory_space=pltpu.VMEM)
    hbm = pl.BlockSpec(memory_space=pltpu.HBM)
    out = jax.ShapeDtypeStruct((ROWS, D), F32)
    sums = pl.pallas_call(
        kernel,
        out_shape=(out, out),
        in_specs=[vmem] * 2 + [hbm] * 2,
        out_specs=(vmem, vmem),
        scratch_shapes=[
            pltpu.VMEM((ROWS, D), BF16),
            pltpu.VMEM((ROWS, D), BF16),
            pltpu.VMEM((ROWS, D), BF16),
            pltpu.VMEM((ROWS, D), BF16),
            pltpu.VMEM((2 * ROWS, D), BF16),
            pltpu.VMEM((3, 2 * ROWS, D), BF16),
            pltpu.VMEM((2 * ROWS, D), BF16),
            pltpu.VMEM((ROWS, D), BF16),
            pltpu.VMEM((4 * ROWS, D), BF16),
            pltpu.VMEM((4 * ROWS, D), BF16),
            pltpu.VMEM((2 * ROWS, D), F32),
            pltpu.VMEM((ROWS, D), F32),
            pltpu.VMEM((3, 2 * ROWS, D), F32),
            pltpu.VMEM((ROWS, D), F32),
            pltpu.VMEM((4, ROWS, D), BF16),
            pltpu.VMEM((4, ROWS, D), BF16),
            pltpu.VMEM((4, ROWS, D), BF16),
            pltpu.VMEM((4, ROWS, D), BF16),
            pltpu.VMEM((ROWS, D), BF16),
            pltpu.VMEM((ROWS, D), BF16),
            pltpu.VMEM((2, ROWS, 1), F32),
            pltpu.SemaphoreType.DMA((4,)),
            pltpu.SemaphoreType.DMA((2, 14 * C + 10)),
            pltpu.SemaphoreType.REGULAR((4,)),
        ],
        compiler_params=pltpu.CompilerParams(
            collective_id=0, has_side_effects=True, vmem_limit_bytes=40 * 1024 * 1024
        ),
        cost_estimate=pl.CostEstimate(
            flops=2_600_000_000, bytes_accessed=2_000_000, transcendentals=500_000
        ),
        name="pairs",
    )(
        log_temp.reshape(1, 1),
        bias.reshape(1, 1),
        pltpu.with_memory_space_constraint(images, pltpu.HBM),
        pltpu.with_memory_space_constraint(texts, pltpu.HBM),
    )
    return pl.pallas_call(
        store,
        out_shape=(out, out),
        in_specs=[vmem, vmem],
        out_specs=(hbm, hbm),
        scratch_shapes=[pltpu.SemaphoreType.DMA((2,))],
        compiler_params=pltpu.CompilerParams(vmem_limit_bytes=2 * 1024 * 1024),
        name="store",
    )(*sums)


def solution(mesh):
    return jax.shard_map(
        per_device,
        mesh=mesh,
        in_specs=(P(("grp", "blk"), None), P(("grp", "blk"), None), P(), P()),
        out_specs=(P(("grp", "blk"), None), P(("grp", "blk"), None)),
        check_vma=False,
    )
```
